256 devices in a mesh: lev: 8 (over x_lo, y), tile: 32 (over x_hi, z, core).
Axes of the slice: x: 4 (x_hi: 2, x_lo: 2; x = x_hi * 2 + x_lo), y: 4, z: 8, core: 2. Of those that a mesh axis runs over, the one named last changes fastest.
Arguments:
- cotangent: bfloat16 [72, 96, 32768], P('lev', None, 'tile'), may hold values from -6 to 6
- particles: bfloat16 [72, 96, 32768], P('lev', None, 'tile'), may hold values from 0.049804688 to 2
- coag_rate: float32 [72], P('lev'), may hold values from 0.004 to 0.015
- courant: float32 [2, 72, 32768], P(None, 'lev', 'tile'), may hold values from 0.05 to 0.45
- offsets: int32 [2, 32768], P(None, 'tile'), may hold values from -2 to 2
- mass_flux: bfloat16 [72, 72, 32768], P(None, None, ('tile', 'lev')), may hold values from -0.75 to 0.75
- cloud_top: int32 [32768], P(('tile', 'lev')), may hold values from 18 to 71
Outputs:
- result: float32 [72, 96, 32768], P(None, None, ('tile', 'lev'))
The draws below stay inside these ranges and needn't reach their ends.
All inputs are finite; a program needn't handle non-finite values.
Results may differ from the reference program's by a relative error of at most 0.0029.
Values may be sent and summed in bfloat16 or wider, within the bound.
No kernel may reach another device: no remote copies, remote signals or barrier semaphores. Data moves between devices by JAX's collectives and lax.ppermute only.
A program may use at most 64 MiB of HBM per device.

```python
import math
import jax
import jax.numpy as jnp
from jax import lax

L = 72
NB = 96
NX = 128
REACH = 2
NY = 256
NCOL = 32768


def place_ends(values, own_key, least, high):
    dims = values.shape
    place = [jax.random.randint(jax.random.fold_in(own_key, axis), (), 0, dims[axis]) for axis in range(len(dims))]
    values = values.at[tuple(place)].set(least)
    longest = dims.index(max(dims))
    place[longest] = (place[longest] + 1) % dims[longest]
    return values.at[tuple(place)].set(high)


def block_scale(rng, shape, split, low, largest):
    factor_of = 1.0
    for position, blocks in split:
        heights = jax.random.uniform(jax.random.fold_in(jax.random.fold_in(rng, 6), position), (blocks,), jnp.float32, low / len(split), largest / len(split))
        factor_of = factor_of * jnp.repeat(jnp.exp(heights), shape[position] // blocks).reshape((-1,) + (1,) * (len(shape) - 1 - position))
    return factor_of


def scatter_about(own_key, extent, width, reach, split=(), held_as=jnp.bfloat16):
    drawn = width * jax.random.normal(own_key, extent, jnp.float32)
    if split:
        drawn = drawn * block_scale(own_key, extent, split, -0.22, 0.18)
    return jnp.clip(drawn, -reach, reach).astype(held_as)


def setup_inputs(seed: int = 0) -> dict:
    splits = jax.random.split(jax.random.key(seed), 8)
    return {
        "cotangent": scatter_about(splits[0], (L, NB, NCOL), 1.0, 6.0, ((0, 8), (2, 32))),
        "particles": jnp.clip(jnp.exp(math.log(2.0) - 3.6927934 * jax.random.uniform(splits[1], (L, NB, NCOL), jnp.float32) ** block_scale(splits[1], (L, NB, NCOL), ((0, 8), (2, 32)), -0.2, 0.2)), 0.049804688, 2.0).astype(jnp.bfloat16),
        "coag_rate": jnp.clip(jnp.exp(math.log(0.015) - 1.3217558 * jax.random.uniform(splits[2], (L,), jnp.float32) ** block_scale(splits[2], (L,), ((0, 8),), -0.2, 0.2)), 0.004, 0.015),
        "courant": jnp.clip(0.05 + 0.39999999 * jax.random.uniform(splits[3], (2, L, NCOL), jnp.float32) ** block_scale(splits[3], (2, L, NCOL), ((1, 8), (2, 32)), -0.2, 0.2), 0.05, 0.45),
        "offsets": place_ends(jax.random.randint(splits[4], (2, NCOL), -REACH, REACH + 1), jax.random.fold_in(splits[4], 1), -REACH, REACH).astype(jnp.int32),
        "mass_flux": scatter_about(splits[5], (L, L, NCOL), L ** -0.5, 0.75, ((2, 256),)),
        "cloud_top": place_ends(jax.random.randint(splits[6], (NCOL,), L // 4, L), jax.random.fold_in(splits[6], 1), L // 4, L - 1).astype(jnp.int32),
    }


def build_tables():
    length = 2 * NB
    bin_index = lax.broadcasted_iota(jnp.int32, (length, NB), 1)
    freq_index = lax.broadcasted_iota(jnp.int32, (length, NB), 0)
    phase_angle = ((bin_index * freq_index) % length).astype(jnp.float32) * (2.0 * math.pi / length)
    fwd_cos = jnp.cos(phase_angle).astype(jnp.bfloat16)
    fwd_sin = (-jnp.sin(phase_angle)).astype(jnp.bfloat16)
    inv_cos = (jnp.transpose(jnp.cos(phase_angle)) / length).astype(jnp.bfloat16)
    inv_sin = (jnp.transpose(-jnp.sin(phase_angle)) / length).astype(jnp.bfloat16)
    return fwd_cos, fwd_sin, inv_cos, inv_sin


def coagulate_level(gradient, particles, coefficient, tables):
    fwd_cos, fwd_sin, inv_cos, inv_sin = tables
    grad_re = jnp.dot(fwd_cos, gradient, preferred_element_type=jnp.float32)
    grad_im = jnp.dot(fwd_sin, gradient, preferred_element_type=jnp.float32)
    mass_re = jnp.dot(fwd_cos, particles, preferred_element_type=jnp.float32)
    mass_im = jnp.dot(fwd_sin, particles, preferred_element_type=jnp.float32)
    prod_re = (mass_re * grad_re + mass_im * grad_im).astype(jnp.bfloat16)
    prod_im = (mass_re * grad_im - mass_im * grad_re).astype(jnp.bfloat16)
    correlation = jnp.dot(inv_cos, prod_re, preferred_element_type=jnp.float32) + jnp.dot(inv_sin, prod_im, preferred_element_type=jnp.float32)
    grad_wide = gradient.astype(jnp.float32)
    mass_wide = particles.astype(jnp.float32)
    total_mass = jnp.sum(mass_wide, axis=0)
    inner = jnp.sum(grad_wide * mass_wide, axis=0)
    return grad_wide + coefficient * (correlation - grad_wide * total_mass - inner)


def remap_level(adjoint, cour_grid, shift_grid):
    shift_y = shift_grid[0]
    shift_x = shift_grid[1]
    pad_y = jnp.pad(adjoint, ((0, 0), (REACH, REACH), (0, 0)))
    pad_x = jnp.pad(adjoint, ((0, 0), (0, 0), (REACH, REACH)))
    along_y = jnp.zeros_like(adjoint)
    along_x = jnp.zeros_like(adjoint)
    for upwind in range(-REACH, REACH + 1):
        along_y = along_y + jnp.where(shift_y == upwind, pad_y[:, REACH + upwind:REACH + upwind + NY, :], 0.0)
        along_x = along_x + jnp.where(shift_x == upwind, pad_x[:, :, REACH + upwind:REACH + upwind + NX], 0.0)
    cour_y = cour_grid[0]
    cour_x = cour_grid[1]
    return adjoint * (1.0 - cour_y - cour_x) + cour_y * along_y + cour_x * along_x


def reference(cotangent, particles, coag_rate, courant, offsets, mass_flux, cloud_top):
    shift_grid = offsets.reshape(2, NY, NX)
    tables = build_tables()

    def level_step(pieces):
        gradient, amounts, coefficient, cour_level = pieces
        adjoint = coagulate_level(gradient, amounts, coefficient, tables)
        remapped = remap_level(adjoint.reshape(NB, NY, NX), cour_level.reshape(2, NY, NX), shift_grid)
        return remapped.reshape(NB, NCOL).astype(jnp.bfloat16)

    remapped = lax.map(level_step, (cotangent, particles, coag_rate, jnp.moveaxis(courant, 1, 0)))
    level_ids = jnp.arange(L, dtype=jnp.int32)
    inside = level_ids[:, None] <= cloud_top[None, :]
    masked = jnp.where(inside[:, None, :] & inside[None, :, :], mass_flux, jnp.zeros_like(mass_flux))
    row_data = jnp.moveaxis(remapped.reshape(L, NB, NY, NX), 2, 0)
    row_flux = jnp.moveaxis(masked.reshape(L, L, NY, NX), 2, 0)

    def column_step(pieces):
        column_data, flux_rows = pieces
        mixing = jnp.einsum('obc,oic->ibc', column_data.astype(jnp.float32), flux_rows.astype(jnp.float32), precision=lax.Precision.HIGHEST)
        return column_data.astype(jnp.float32) + mixing

    result = lax.map(column_step, (row_data, row_flux))
    return jnp.moveaxis(result, 0, 2).reshape(L, NB, NCOL)
```

```python
import functools
import math

import jax
import jax.numpy as jnp
import ml_dtypes
import numpy as np
from jax import lax
from jax.experimental import pallas as pl
from jax.experimental.pallas import tpu as pltpu
from jax.sharding import PartitionSpec as P

NX = 128
ROWS = 8
REACH = 2
BINS = 96
LOCAL = 9
LEVELS = 72
PEERS = 8
STEP = 3
SUB = 4
MIX = 12
BF16 = jnp.bfloat16
F32 = jnp.float32


def tables():
    length = 2 * BINS
    freq, bins = np.arange(BINS)[:, None], np.arange(BINS)[None, :]
    theta = 2.0 * math.pi * ((freq * bins) % length) / length
    nyquist = 1.0 - 2.0 * (np.arange(BINS) % 2)
    cos, sin = np.cos(theta), -np.sin(theta)
    sin[0] = nyquist
    forward = np.concatenate([cos, sin], axis=0)
    weight = np.where(np.arange(BINS) == 0, 1.0, 2.0)[:, None] / length
    inverse = np.concatenate([cos * weight, sin * weight], axis=0).T
    return forward.astype(ml_dtypes.bfloat16), np.ascontiguousarray(inverse).astype(ml_dtypes.bfloat16)


def adjoint_of(forward, inverse, gradient, amounts, coefficient):
    grad_spec = jnp.dot(forward, gradient, preferred_element_type=F32)
    mass_spec = jnp.dot(forward, amounts, preferred_element_type=F32)
    grad_re, grad_im = grad_spec[:BINS], grad_spec[BINS:]
    mass_re, mass_im = mass_spec[:BINS], mass_spec[BINS:]
    total_mass = mass_re[0:1]
    first = lax.broadcasted_iota(jnp.int32, (8, gradient.shape[1]), 0) == 0
    re_re, im_im = mass_re * grad_re, mass_im * grad_im
    prod_re = re_re + im_im
    prod_im = mass_re * grad_im - mass_im * grad_re
    prod_re = jnp.concatenate([jnp.where(first, re_re[:8], prod_re[:8]), prod_re[8:]], axis=0)
    prod_im = jnp.concatenate([jnp.where(first, im_im[:8], prod_im[:8]), prod_im[8:]], axis=0)
    prod = jnp.concatenate([prod_re.astype(BF16), prod_im.astype(BF16)], axis=0)
    correlation = jnp.dot(inverse, prod, preferred_element_type=F32)
    grad_wide = gradient.astype(F32)
    inner = jnp.sum(grad_wide * amounts.astype(F32), axis=0, keepdims=True)
    return grad_wide + coefficient * (correlation - grad_wide * total_mass - inner)


def edge_kernel(rate, forward, inverse, grad_lo, mass_lo, grad_hi, mass_hi, wide, lo, hi):
    step = pl.program_id(0)

    def level(j, carry):
        coefficient = rate[step * STEP + j]
        for side, (grad, mass, out) in enumerate(((grad_lo, mass_lo, lo), (grad_hi, mass_hi, hi))):
            adjoint = adjoint_of(forward[...], inverse[...], grad[j], mass[j], coefficient)
            wide[j, :, side * 256 : (side + 1) * 256] = adjoint
            out[j] = adjoint.astype(BF16)
        return carry

    lax.fori_loop(0, STEP, level, 0)


def inner_kernel(rate, forward, inverse, grad_lo, mass_lo, grad_hi, mass_hi, wide, courant, offsets, ready, partial, cells):
    step = pl.program_id(0)
    lane = lax.broadcasted_iota(jnp.int32, (1, NX), 1)

    def level(j, carry):
        coefficient = rate[step * STEP + j]
        cells[:, 0:256] = wide[j, :, 0:256]
        cells[:, 768:1024] = wide[j, :, 256:512]
        for side, (grad, mass) in enumerate(((grad_lo, mass_lo), (grad_hi, mass_hi))):
            adjoint = adjoint_of(forward[...], inverse[...], grad[j], mass[j], coefficient)
            cells[:, (side + 1) * 256 : (side + 2) * 256] = adjoint
        for row in range(ROWS):
            span = slice(row * NX, (row + 1) * NX)
            cour_y, cour_x = courant[j, 0:1, span], courant[j, 1:2, span]
            shift_y, shift_x = offsets[0:1, span], offsets[1:2, span]
            centre = cells[:, span]
            total = centre * (1.0 - cour_y - cour_x)
            for upwind in range(-REACH, REACH + 1):
                if 0 <= row + upwind < ROWS:
                    weight = jnp.where(shift_y == upwind, cour_y, 0.0)
                    near = slice((row + upwind) * NX, (row + upwind + 1) * NX)
                    total = total + cells[:, near] * weight
            place = lane + shift_x
            weight = jnp.where((place >= 0) & (place < NX), cour_x, 0.0)
            place = jnp.broadcast_to(jnp.clip(place, 0, NX - 1), centre.shape)
            along_x = jnp.take_along_axis(centre, place, axis=1, mode="promise_in_bounds")
            total = total + along_x * weight
            if 2 <= row < 6:
                ready[row - 2, j] = total.astype(BF16)
            else:
                partial[row if row < 2 else row - 4, j] = total
        return carry

    lax.fori_loop(0, STEP, level, 0)


def finish_kernel(me, ready, partial, above, below, courant, offsets, *outs):
    def level(j, carry):
        for turn in range(PEERS):
            row = jnp.bitwise_xor(me[0], turn)
            out = outs[turn]

            @pl.when((row >= 2) & (row < 6))
            def _():
                out[j] = ready[row - 2, j]

            for edge, (place, terms) in enumerate(
                (
                    (0, ((above, 0, -2), (above, 1, -1))),
                    (1, ((above, 1, -2),)),
                    (6, ((below, 0, 2),)),
                    (7, ((below, 0, 1), (below, 1, 2))),
                )
            ):

                @pl.when(row == place)
                def _(edge=edge, place=place, terms=terms):
                    span = slice(place * NX, (place + 1) * NX)
                    cour_y, shift_y = courant[j, 0:1, span], offsets[0:1, span]
                    total = partial[edge, j]
                    for ref, line, upwind in terms:
                        weight = jnp.where(shift_y == upwind, cour_y, 0.0)
                        total = total + ref[j, :, line * NX : (line + 1) * NX].astype(F32) * weight
                    out[j] = total.astype(BF16)

        return carry

    lax.fori_loop(0, STEP, level, 0)


def mix_kernel(has_acc, source, flux, cloud_top, block, *refs):
    acc = refs[0] if has_acc else None
    out, weights, wide = refs[-3:]
    step = pl.program_id(0)

    @pl.when(step == 0)
    def _():
        top = cloud_top[...]
        levels = lax.broadcasted_iota(jnp.int32, (LEVELS, NX), 0)
        inside = levels <= top
        for o in range(LOCAL):
            level = source[0] * LOCAL + o
            kept = jnp.where(inside & (level <= top), flux[o].astype(F32), 0.0)
            weights[o] = kept + jnp.where(levels == level, 1.0, 0.0)
            wide[o] = block[o].astype(F32)

    def some(q, carry):
        first = step * MIX + q * SUB
        sums = [acc[q * SUB + n] if has_acc else None for n in range(SUB)]
        for o in range(LOCAL):
            data = wide[o]
            for n in range(SUB):
                term = data * weights[o, pl.ds(first + n, 1), :]
                sums[n] = term if sums[n] is None else sums[n] + term
        for n in range(SUB):
            out[q * SUB + n] = sums[n]
        return carry

    lax.fori_loop(0, MIX // SUB, some, 0)


def mix(source, flux, cloud_top, block, acc):
    has_acc = acc is not None
    rows = pl.BlockSpec((MIX, BINS, NX), lambda i, s: (i, 0, 0))
    in_specs = [
        pl.BlockSpec((LOCAL, LEVELS, NX), lambda i, s: (s[0], 0, 0)),
        pl.BlockSpec((1, NX), lambda i, s: (0, 0)),
        pl.BlockSpec((LOCAL, BINS, NX), lambda i, s: (0, 0, 0)),
    ]
    return pl.pallas_call(
        functools.partial(mix_kernel, has_acc),
        out_shape=jax.ShapeDtypeStruct((LEVELS, BINS, NX), F32),
        grid_spec=pltpu.PrefetchScalarGridSpec(
            num_scalar_prefetch=1,
            grid=(LEVELS // MIX,),
            in_specs=in_specs + ([rows] if has_acc else []),
            out_specs=rows,
            scratch_shapes=[pltpu.VMEM((LOCAL, LEVELS, NX), F32), pltpu.VMEM((LOCAL, BINS, NX), F32)],
        ),
        input_output_aliases={4: 0} if has_acc else {},
        compiler_params=pltpu.CompilerParams(vmem_limit_bytes=24 << 20),
        cost_estimate=pl.CostEstimate(flops=4_000_000, bytes_accessed=7_000_000, transcendentals=0),
        name="mix",
    )(source, flux, cloud_top, block, *([acc] if has_acc else []))


def whole(shape):
    return pl.BlockSpec(shape, lambda i: (0,) * len(shape))


def body(cotangent, particles, coag_rate, courant, offsets, mass_flux, cloud_top):
    forward, inverse = (jnp.asarray(t) for t in tables())
    courant = jnp.moveaxis(courant, 1, 0)
    me = lax.axis_index("lev").astype(jnp.int32)
    smem = pl.BlockSpec(memory_space=pltpu.SMEM)
    params = pltpu.CompilerParams(vmem_limit_bytes=40 << 20)

    def columns(n):
        return pl.BlockSpec((STEP, BINS, 256), lambda i: (i, 0, n))

    halo_shape = jax.ShapeDtypeStruct((LOCAL, BINS, 256), BF16)
    halo_spec = pl.BlockSpec((STEP, BINS, 256), lambda i: (i, 0, 0))
    wide_spec = pl.BlockSpec((STEP, BINS, 512), lambda i: (i, 0, 0))
    row_spec = pl.BlockSpec((4, STEP, BINS, NX), lambda i: (0, i, 0, 0))
    courant_spec = pl.BlockSpec((STEP, 2, 1024), lambda i: (i, 0, 0))
    table_specs = [smem, whole((2 * BINS, BINS)), whole((BINS, 2 * BINS))]
    wide, lo, hi = pl.pallas_call(
        edge_kernel,
        grid=(LOCAL // STEP,),
        out_shape=(jax.ShapeDtypeStruct((LOCAL, BINS, 512), F32), halo_shape, halo_shape),
        in_specs=table_specs + [columns(0), columns(0), columns(3), columns(3)],
        out_specs=(wide_spec, halo_spec, halo_spec),
        compiler_params=params,
        cost_estimate=pl.CostEstimate(flops=600_000_000, bytes_accessed=5_000_000, transcendentals=0),
        name="edge",
    )(coag_rate, forward, inverse, cotangent, particles, cotangent, particles)
    count = lax.axis_size("tile")
    above = lax.ppermute(hi, "tile", [(i, i + 1) for i in range(count - 1)])
    below = lax.ppermute(lo, "tile", [(i + 1, i) for i in range(count - 1)])
    ready, partial = pl.pallas_call(
        inner_kernel,
        grid=(LOCAL // STEP,),
        out_shape=(
            jax.ShapeDtypeStruct((4, LOCAL, BINS, NX), BF16),
            jax.ShapeDtypeStruct((4, LOCAL, BINS, NX), F32),
        ),
        in_specs=table_specs
        + [columns(1), columns(1), columns(2), columns(2), wide_spec, courant_spec, whole((2, 1024))],
        out_specs=(row_spec, row_spec),
        scratch_shapes=[pltpu.VMEM((BINS, 1024), F32)],
        compiler_params=params,
        cost_estimate=pl.CostEstimate(flops=600_000_000, bytes_accessed=8_000_000, transcendentals=0),
        name="inner",
    )(coag_rate, forward, inverse, cotangent, particles, cotangent, particles, wide, courant, offsets)
    block_spec = pl.BlockSpec((STEP, BINS, NX), lambda i: (i, 0, 0))
    blocks = pl.pallas_call(
        finish_kernel,
        grid=(LOCAL // STEP,),
        out_shape=(jax.ShapeDtypeStruct((LOCAL, BINS, NX), BF16),) * PEERS,
        in_specs=[smem, row_spec, row_spec, halo_spec, halo_spec, courant_spec, whole((2, 1024))],
        out_specs=(block_spec,) * PEERS,
        compiler_params=params,
        cost_estimate=pl.CostEstimate(flops=2_000_000, bytes_accessed=5_000_000, transcendentals=0),
        name="finish",
    )(me[None], ready, partial, above, below, courant, offsets)
    top = cloud_top[None, :]
    arrived = [blocks[0]] + [
        lax.ppermute(blocks[turn], "lev", [(i, i ^ turn) for i in range(PEERS)]) for turn in range(1, PEERS)
    ]
    acc = None
    for turn in (0, 4, 1, 3, 2, 5, 7, 6):
        acc = mix(jnp.bitwise_xor(me, turn)[None], mass_flux, top, arrived[turn], acc)
    return acc


def solution(mesh):
    placed = (
        P("lev", None, "tile"),
        P("lev", None, "tile"),
        P("lev"),
        P(None, "lev", "tile"),
        P(None, "tile"),
        P(None, None, ("tile", "lev")),
        P(("tile", "lev")),
    )
    return jax.shard_map(
        body, mesh=mesh, in_specs=placed, out_specs=P(None, None, ("tile", "lev")), check_vma=False
    )
```

```python
import functools
import math

import jax
import jax.numpy as jnp
import ml_dtypes
import numpy as np
from jax import lax
from jax.experimental import pallas as pl
from jax.experimental.pallas import tpu as pltpu
from jax.sharding import PartitionSpec as P

NX = 128
ROWS = 8
REACH = 2
BINS = 96
LOCAL = 9
LEVELS = 72
PEERS = 8
STEP = 3
HALF = 512
SUB = 6
OUTER = ((0, -2), (0, -1), (1, -2), (6, 2), (7, 1), (7, 2))
PART = 48
ORDER = (0, 4, 3, 5, 2, 6, 7, 1)
AHEAD = 8
BF16 = jnp.bfloat16
F32 = jnp.float32


def tables():
    length = 2 * BINS
    freq, bins = np.arange(BINS)[:, None], np.arange(BINS)[None, :]
    theta = 2.0 * math.pi * ((freq * bins) % length) / length
    nyquist = 1.0 - 2.0 * (np.arange(BINS) % 2)
    cos, sin = np.cos(theta), -np.sin(theta)
    sin[0] = nyquist
    forward = np.concatenate([cos, sin], axis=0)
    weight = np.where(np.arange(BINS) == 0, 1.0, 2.0)[:, None] / length
    inverse = np.concatenate([cos * weight, sin * weight], axis=0).T
    return forward.astype(ml_dtypes.bfloat16), np.ascontiguousarray(inverse).astype(ml_dtypes.bfloat16)


def adjoint_of(forward, inverse, gradient, amounts, coefficient):
    grad_spec = jnp.dot(forward, gradient, preferred_element_type=F32)
    mass_spec = jnp.dot(forward, amounts, preferred_element_type=F32)
    grad_re, grad_im = grad_spec[:BINS], grad_spec[BINS:]
    mass_re, mass_im = mass_spec[:BINS], mass_spec[BINS:]
    total_mass = mass_re[0:1]
    first = lax.broadcasted_iota(jnp.int32, (8, gradient.shape[1]), 0) == 0
    re_re, im_im = mass_re * grad_re, mass_im * grad_im
    prod_re = re_re + im_im
    prod_im = mass_re * grad_im - mass_im * grad_re
    prod_re = jnp.concatenate([jnp.where(first, re_re[:8], prod_re[:8]), prod_re[8:]], axis=0)
    prod_im = jnp.concatenate([jnp.where(first, im_im[:8], prod_im[:8]), prod_im[8:]], axis=0)
    prod = jnp.concatenate([prod_re.astype(BF16), prod_im.astype(BF16)], axis=0)
    correlation = jnp.dot(inverse, prod, preferred_element_type=F32)
    grad_wide = gradient.astype(F32)
    inner = jnp.sum(grad_wide * amounts.astype(F32), axis=0, keepdims=True)
    return grad_wide + coefficient * (correlation - grad_wide * total_mass - inner)


def group_copies(pairs, sems, group, low):
    span = pl.ds(group * STEP, STEP)
    width = HALF // len(low)
    return [
        pltpu.make_async_copy(
            source.at[span, :, start : start + width],
            target.at[span, :, side * width : (side + 1) * width],
            sems.at[group, n, side],
        )
        for n, (source, target) in enumerate(pairs)
        for side, start in enumerate(low)
    ]


def begin(copies):
    for copy in copies:
        copy.start()


def finish_copies(copies):
    for copy in copies:
        copy.wait()


def edge_kernel(rate, forward, inverse, cotangent, particles, wide, lo, hi, *scratch):
    grad, mass, forward_in, inverse_in, rate_in, sems, small_sems = scratch
    pairs = ((cotangent, grad), (particles, mass))
    small = [
        pltpu.make_async_copy(source, target, small_sems.at[n])
        for n, (source, target) in enumerate(((rate, rate_in), (forward, forward_in), (inverse, inverse_in)))
    ]
    begin(group_copies(pairs, sems, 0, (0, 768)) + small)
    finish_copies(small)

    def some(group, carry):
        finish_copies(group_copies(pairs, sems, group, (0, 768)))

        @pl.when(group < LOCAL // STEP - 1)
        def _():
            begin(group_copies(pairs, sems, group + 1, (0, 768)))

        for j in range(STEP):
            level = group * STEP + j
            adjoint = adjoint_of(forward_in[...], inverse_in[...], grad[level], mass[level], rate_in[level])
            wide[level] = adjoint
            lo[level] = adjoint[:, :256].astype(BF16)
            hi[level] = adjoint[:, 256:].astype(BF16)
        return carry

    lax.fori_loop(0, LOCAL // STEP, some, 0)


def inner_kernel(rate, forward, inverse, cotangent, particles, wide, courant, offsets, ready, partial, outer, *scratch):
    grad, mass, forward_in, inverse_in, courant_in, offsets_in, cells, sems, small_sems = scratch
    lane = lax.broadcasted_iota(jnp.int32, (1, NX), 1)
    pairs = ((cotangent, grad), (particles, mass))
    ins = ((forward, forward_in), (inverse, inverse_in), (courant, courant_in), (offsets, offsets_in))
    small = [pltpu.make_async_copy(source, target, small_sems.at[n]) for n, (source, target) in enumerate(ins)]
    begin(group_copies(pairs, sems, 0, (256,)) + small)
    finish_copies(small)
    for n, (row, upwind) in enumerate(OUTER):
        span = slice(row * NX, (row + 1) * NX)
        outer[n] = jnp.where(offsets_in[0:1, span] == upwind, courant_in[:, 0, span], 0.0)

    def near(level, j, row):
        if 2 <= row < 6:
            return cells[j, :, (row - 2) * NX : (row - 1) * NX]
        edge = row if row < 2 else row - 4
        return wide[level, :, edge * NX : (edge + 1) * NX]

    def some(group, carry):
        finish_copies(group_copies(pairs, sems, group, (256,)))

        @pl.when(group < LOCAL // STEP - 1)
        def _():
            begin(group_copies(pairs, sems, group + 1, (256,)))

        for j in range(STEP):
            level = group * STEP + j
            cells[j] = adjoint_of(forward_in[...], inverse_in[...], grad[level], mass[level], rate[level])
        for j in range(STEP):
            level = group * STEP + j
            for row in range(ROWS):
                span = slice(row * NX, (row + 1) * NX)
                cour_y, cour_x = courant_in[level, 0:1, span], courant_in[level, 1:2, span]
                shift_y, shift_x = offsets_in[0:1, span], offsets_in[1:2, span]
                centre = near(level, j, row)
                still = jnp.where(shift_y == 0, cour_y, 0.0)
                total = centre * (1.0 - cour_y - cour_x + still)
                for upwind in (-2, -1, 1, 2):
                    if 0 <= row + upwind < ROWS:
                        weight = jnp.where(shift_y == upwind, cour_y, 0.0)
                        total = total + near(level, j, row + upwind) * weight
                place = lane + shift_x
                weight = jnp.where((place >= 0) & (place < NX), cour_x, 0.0)
                place = jnp.broadcast_to(jnp.clip(place, 0, NX - 1), centre.shape)
                along_x = jnp.take_along_axis(centre, place, axis=1, mode="promise_in_bounds")
                total = total + along_x * weight
                if 2 <= row < 6:
                    ready[row - 2, level] = total.astype(BF16)
                else:
                    partial[row if row < 2 else row - 4, level] = total
        return carry

    lax.fori_loop(0, LOCAL // STEP, some, 0)


def finish_kernel(ready, partial, above, below, outer, *outs):
    me = lax.axis_index("lev")
    edges = (
        (0, ((above, 0, 0), (above, 1, 1))),
        (1, ((above, 1, 2),)),
        (6, ((below, 0, 3),)),
        (7, ((below, 0, 4), (below, 1, 5))),
    )

    def inside(row, out):
        for j in range(LOCAL):
            out[j] = ready[row - 2, j]

    def outside(edge, terms, out):
        for j in range(LOCAL):
            total = partial[edge, j]
            for ref, line, n in terms:
                total = total + ref[j, :, line * NX : (line + 1) * NX].astype(F32) * outer[n, j : j + 1]
            out[j] = total.astype(BF16)

    for turn in range(PEERS):
        row = jnp.bitwise_xor(me, turn)
        pl.when((row >= 2) & (row < 6))(functools.partial(inside, row, outs[turn]))
        for edge, (place, terms) in enumerate(edges):
            pl.when(row == place)(functools.partial(outside, edge, terms, outs[turn]))


def mix_kernel(first, last, waits, source, flux, cloud_top, block, *refs):
    refs = list(refs)
    acc = None if first else refs.pop(0)
    if waits:
        del refs[0], refs[1]
    out, weights, wide = refs[:3]
    top = cloud_top[...]
    levels = lax.broadcasted_iota(jnp.int32, (LEVELS, NX), 0)
    inside = levels <= top
    for o in range(LOCAL):
        level = source[0] * LOCAL + o
        kept = jnp.where(inside & (level <= top), flux[level].astype(F32), 0.0)
        weights[o] = kept + jnp.where(levels == level, 1.0, 0.0)
        wide[o] = block[o].astype(F32)
    held = refs[3] if last else out

    def to_out(q):
        span = pl.ds(q * SUB, SUB)
        return pltpu.make_async_copy(held.at[span], out.at[span], refs[4].at[q])

    def some(q, carry):
        row = q * SUB
        for low in range(0, BINS, PART):
            span = slice(low, low + PART)
            sums = [None if first else acc[row + n, span] for n in range(SUB)]
            for o in range(LOCAL):
                data = wide[o, span]
                for n in range(SUB):
                    term = data * weights[o, pl.ds(row + n, 1), :]
                    sums[n] = term if sums[n] is None else sums[n] + term
            for n in range(SUB):
                held[row + n, span] = sums[n]
        if last:
            to_out(q).start()
        return carry

    lax.fori_loop(0, LEVELS // SUB, some, 0)
    if last:

        def finished(q, carry):
            to_out(q).wait()
            return carry

        lax.fori_loop(0, LEVELS // SUB, finished, 0)


def near_core(x):
    return pltpu.with_memory_space_constraint(x, pltpu.VMEM)


VM = pl.BlockSpec(memory_space=pltpu.VMEM)
SM = pl.BlockSpec(memory_space=pltpu.SMEM)
FAR = pl.BlockSpec(memory_space=pltpu.HBM)


def mix(source, flux, cloud_top, block, acc, waiting, last):
    first = acc is None
    shape = (LEVELS, BINS, NX)
    scratch = [pltpu.VMEM((LOCAL, LEVELS, NX), F32), pltpu.VMEM((LOCAL, BINS, NX), F32)]
    if last:
        scratch += [pltpu.VMEM(shape, F32), pltpu.SemaphoreType.DMA((LEVELS // SUB,))]
    chained = [x for x in (acc, waiting) if x is not None]
    outs = [jax.ShapeDtypeStruct(shape, F32) if last else pltpu.VMEM(shape, F32)]
    aliases = {} if first or last else {4: 0}
    if waiting is not None:
        outs.append(pltpu.VMEM(waiting.shape, waiting.dtype))
        aliases[3 + len(chained)] = 1
    made = pl.pallas_call(
        functools.partial(mix_kernel, first, last, waiting is not None),
        out_shape=tuple(outs),
        in_specs=[SM, VM, VM, VM] + [VM] * len(chained),
        out_specs=(FAR if last else VM,) * len(outs),
        scratch_shapes=scratch,
        input_output_aliases=aliases,
        compiler_params=pltpu.CompilerParams(vmem_limit_bytes=12 << 20),
        cost_estimate=pl.CostEstimate(flops=1500000000, bytes_accessed=7000000, transcendentals=0),
        name="mix",
    )(source, near_core(flux), near_core(cloud_top), near_core(block), *chained)
    return made[0], made[-1]


def body(cotangent, particles, coag_rate, courant, offsets, mass_flux, cloud_top):
    forward, inverse = (jnp.asarray(t) for t in tables())
    courant = jnp.moveaxis(courant, 1, 0)
    me = lax.axis_index("lev").astype(jnp.int32)
    params = pltpu.CompilerParams(vmem_limit_bytes=10 << 20)
    half = pltpu.VMEM((LOCAL, BINS, HALF), BF16)
    quarter = pltpu.VMEM((LOCAL, BINS, 256), BF16)
    table_scratch = [pltpu.VMEM((2 * BINS, BINS), BF16), pltpu.VMEM((BINS, 2 * BINS), BF16)]
    groups = LOCAL // STEP
    far = functools.partial(pltpu.with_memory_space_constraint, memory_space=pltpu.HBM)
    inputs = [far(x) for x in (forward, inverse, cotangent, particles)]
    wide, lo, hi = pl.pallas_call(
        edge_kernel,
        out_shape=(pltpu.VMEM((LOCAL, BINS, HALF), F32), quarter, quarter),
        in_specs=[FAR] * 5,
        out_specs=(VM,) * 3,
        scratch_shapes=[
            half,
            half,
            *table_scratch,
            pltpu.SMEM((LOCAL,), F32),
            pltpu.SemaphoreType.DMA((groups, 2, 2)),
            pltpu.SemaphoreType.DMA((3,)),
        ],
        compiler_params=params,
        cost_estimate=pl.CostEstimate(flops=600_000_000, bytes_accessed=5_000_000, transcendentals=0),
        name="edge",
    )(far(coag_rate), *inputs)
    count = lax.axis_size("tile")
    above = lax.ppermute(hi, "tile", [(i, i + 1) for i in range(count - 1)])
    below = lax.ppermute(lo, "tile", [(i + 1, i) for i in range(count - 1)])
    ready, partial, outer = pl.pallas_call(
        inner_kernel,
        out_shape=(
            pltpu.VMEM((4, LOCAL, BINS, NX), BF16),
            pltpu.VMEM((4, LOCAL, BINS, NX), F32),
            pltpu.VMEM((len(OUTER), LOCAL, NX), F32),
        ),
        in_specs=[SM] + [FAR] * 4 + [VM] + [FAR] * 2,
        out_specs=(VM,) * 3,
        scratch_shapes=[
            half,
            half,
            *table_scratch,
            pltpu.VMEM((LOCAL, 2, 1024), F32),
            pltpu.VMEM((2, 1024), jnp.int32),
            pltpu.VMEM((STEP, BINS, HALF), F32),
            pltpu.SemaphoreType.DMA((groups, 2, 1)),
            pltpu.SemaphoreType.DMA((4,)),
        ],
        compiler_params=params,
        cost_estimate=pl.CostEstimate(flops=600_000_000, bytes_accessed=8_000_000, transcendentals=0),
        name="inner",
    )(coag_rate, *inputs, wide, far(courant), far(offsets))
    blocks = pl.pallas_call(
        finish_kernel,
        out_shape=(pltpu.VMEM((LOCAL, BINS, NX), BF16),) * PEERS,
        in_specs=[VM] * 5,
        out_specs=(VM,) * PEERS,
        compiler_params=params,
        cost_estimate=pl.CostEstimate(flops=2_000_000, bytes_accessed=5_000_000, transcendentals=0),
        name="finish",
    )(ready, partial, near_core(above), near_core(below), outer)
    top = cloud_top[None, :]
    blocks = list(blocks)
    arrived = {0: blocks[0]}

    def send(turn):
        arrived[turn] = lax.ppermute(blocks[turn], "lev", [(i, i ^ turn) for i in range(PEERS)])

    for turn in ORDER[1:AHEAD]:
        send(turn)
    acc = None
    for n, turn in enumerate(ORDER):
        later = ORDER[AHEAD + n] if AHEAD + n < PEERS else None
        waiting = None if later is None else blocks[later]
        source = jnp.bitwise_xor(me, turn)[None]
        acc, passed = mix(source, mass_flux, top, arrived[turn], acc, waiting, n == PEERS - 1)
        if later is not None:
            blocks[later] = passed
            send(later)
    return acc


def solution(mesh):
    placed = (
        P("lev", None, "tile"),
        P("lev", None, "tile"),
        P("lev"),
        P(None, "lev", "tile"),
        P(None, "tile"),
        P(None, None, ("tile", "lev")),
        P(("tile", "lev")),
    )
    return jax.shard_map(
        body, mesh=mesh, in_specs=placed, out_specs=P(None, None, ("tile", "lev")), check_vma=False
    )
```

```python
import functools
import math

import jax
import jax.numpy as jnp
import ml_dtypes
import numpy as np
from jax import lax
from jax.experimental import pallas as pl
from jax.experimental.pallas import tpu as pltpu
from jax.sharding import PartitionSpec as P

NX = 128
ROWS = 8
REACH = 2
BINS = 96
LOCAL = 9
LEVELS = 72
PEERS = 8
STEP = 3
HALF = 512
SUB = 6
OUTER = ((0, -2), (0, -1), (1, -2), (6, 2), (7, 1), (7, 2))
PART = 48
SENDS = (4, 3, 5, 2, 6, 7, 1)
ORDER = (0, 4, 3, 5, 6, 7, 1, 2)
BF16 = jnp.bfloat16
F32 = jnp.float32


def tables():
    length = 2 * BINS
    freq, bins = np.arange(BINS)[:, None], np.arange(BINS)[None, :]
    theta = 2.0 * math.pi * ((freq * bins) % length) / length
    nyquist = 1.0 - 2.0 * (np.arange(BINS) % 2)
    cos, sin = np.cos(theta), -np.sin(theta)
    sin[0] = nyquist
    forward = np.concatenate([cos, sin], axis=0)
    weight = np.where(np.arange(BINS) == 0, 1.0, 2.0)[:, None] / length
    inverse = np.concatenate([cos * weight, sin * weight], axis=0).T
    return forward.astype(ml_dtypes.bfloat16), np.ascontiguousarray(inverse).astype(ml_dtypes.bfloat16)


def adjoint_of(forward, inverse, gradient, amounts, coefficient):
    grad_spec = jnp.dot(forward, gradient, preferred_element_type=F32)
    mass_spec = jnp.dot(forward, amounts, preferred_element_type=F32)
    grad_re, grad_im = grad_spec[:BINS], grad_spec[BINS:]
    mass_re, mass_im = mass_spec[:BINS], mass_spec[BINS:]
    total_mass = mass_re[0:1]
    first = lax.broadcasted_iota(jnp.int32, (8, gradient.shape[1]), 0) == 0
    re_re, im_im = mass_re * grad_re, mass_im * grad_im
    prod_re = re_re + im_im
    prod_im = mass_re * grad_im - mass_im * grad_re
    prod_re = jnp.concatenate([jnp.where(first, re_re[:8], prod_re[:8]), prod_re[8:]], axis=0)
    prod_im = jnp.concatenate([jnp.where(first, im_im[:8], prod_im[:8]), prod_im[8:]], axis=0)
    prod = jnp.concatenate([prod_re.astype(BF16), prod_im.astype(BF16)], axis=0)
    correlation = jnp.dot(inverse, prod, preferred_element_type=F32)
    grad_wide = gradient.astype(F32)
    inner = jnp.sum(grad_wide * amounts.astype(F32), axis=0, keepdims=True)
    return grad_wide + coefficient * (correlation - grad_wide * total_mass - inner)


def group_copies(pairs, sems, group, low):
    span = pl.ds(group * STEP, STEP)
    width = HALF // len(low)
    return [
        pltpu.make_async_copy(
            source.at[span, :, start : start + width],
            target.at[span, :, side * width : (side + 1) * width],
            sems.at[group, n, side],
        )
        for n, (source, target) in enumerate(pairs)
        for side, start in enumerate(low)
    ]


def begin(copies):
    for copy in copies:
        copy.start()


def finish_copies(copies):
    for copy in copies:
        copy.wait()


def edge_kernel(rate, forward, inverse, cotangent, particles, courant, offsets, *refs):
    wide, far_rows, near_rows, grad_mid, mass_mid, forward_in, inverse_in, courant_in, offsets_in = refs[:9]
    grad, mass, rate_in, sems, small_sems, mid_sems = refs[9:]
    even = lax.rem(lax.axis_index("tile"), 2) == 0
    pairs = ((cotangent, grad), (particles, mass))
    small = [
        pltpu.make_async_copy(source, target, small_sems.at[n])
        for n, (source, target) in enumerate(((rate, rate_in), (forward, forward_in), (inverse, inverse_in)))
    ]
    middle = [
        pltpu.make_async_copy(source, target, mid_sems.at[n])
        for n, (source, target) in enumerate(
            (
                (cotangent.at[:, :, 256:768], grad_mid),
                (particles.at[:, :, 256:768], mass_mid),
                (courant, courant_in),
                (offsets, offsets_in),
            )
        )
    ]
    begin(small + group_copies(pairs, sems, 0, (0, 768)))
    finish_copies(small)

    def some(group, carry):
        finish_copies(group_copies(pairs, sems, group, (0, 768)))

        @pl.when(group < LOCAL // STEP - 1)
        def _():
            begin(group_copies(pairs, sems, group + 1, (0, 768)))

        @pl.when(group == LOCAL // STEP - 2)
        def _():
            begin(middle)

        for j in range(STEP):
            level = group * STEP + j
            adjoint = adjoint_of(forward_in[...], inverse_in[...], grad[level], mass[level], rate_in[level])
            wide[level] = adjoint
            lo, hi = adjoint[:, :256], adjoint[:, 256:]
            far_rows[level] = jnp.where(even, lo, hi).astype(BF16)
            near_rows[level] = jnp.where(even, hi, lo).astype(BF16)
        return carry

    lax.fori_loop(0, LOCAL // STEP, some, 0)
    finish_copies(middle)


def inner_kernel(rate, forward, inverse, cotangent, particles, wide, courant, offsets, ready, partial, outer, cells):
    lane = lax.broadcasted_iota(jnp.int32, (1, NX), 1)
    for n, (row, upwind) in enumerate(OUTER):
        span = slice(row * NX, (row + 1) * NX)
        outer[n] = jnp.where(offsets[0:1, span] == upwind, courant[:, 0, span], 0.0)

    def near(level, j, row):
        if 2 <= row < 6:
            return cells[j, :, (row - 2) * NX : (row - 1) * NX]
        edge = row if row < 2 else row - 4
        return wide[level, :, edge * NX : (edge + 1) * NX]

    def some(group, carry):
        for j in range(STEP):
            level = group * STEP + j
            cells[j] = adjoint_of(forward[...], inverse[...], cotangent[level], particles[level], rate[level])
        for j in range(STEP):
            level = group * STEP + j
            for row in range(ROWS):
                span = slice(row * NX, (row + 1) * NX)
                cour_y, cour_x = courant[level, 0:1, span], courant[level, 1:2, span]
                shift_y, shift_x = offsets[0:1, span], offsets[1:2, span]
                centre = near(level, j, row)
                still = jnp.where(shift_y == 0, cour_y, 0.0)
                total = centre * (1.0 - cour_y - cour_x + still)
                for upwind in (-2, -1, 1, 2):
                    if 0 <= row + upwind < ROWS:
                        weight = jnp.where(shift_y == upwind, cour_y, 0.0)
                        total = total + near(level, j, row + upwind) * weight
                place = lane + shift_x
                weight = jnp.where((place >= 0) & (place < NX), cour_x, 0.0)
                place = jnp.broadcast_to(jnp.clip(place, 0, NX - 1), centre.shape)
                along_x = jnp.take_along_axis(centre, place, axis=1, mode="promise_in_bounds")
                total = total + along_x * weight
                if 2 <= row < 6:
                    ready[row - 2, level] = total.astype(BF16)
                else:
                    partial[row if row < 2 else row - 4, level] = total
        return carry

    lax.fori_loop(0, LOCAL // STEP, some, 0)


def finish_kernel(ready, partial, far_rows, near_rows, outer, *outs):
    me = lax.axis_index("lev")
    even = lax.rem(lax.axis_index("tile"), 2) == 0

    def beside(upward, j, line):
        span = slice(line * NX, (line + 1) * NX)
        return jnp.where(even == upward, far_rows[j, :, span], near_rows[j, :, span]).astype(F32)

    edges = (
        (0, ((True, 0, 0), (True, 1, 1))),
        (1, ((True, 1, 2),)),
        (6, ((False, 0, 3),)),
        (7, ((False, 0, 4), (False, 1, 5))),
    )

    def inside(row, out):
        for j in range(LOCAL):
            out[j] = ready[row - 2, j]

    def outside(edge, terms, out):
        for j in range(LOCAL):
            total = partial[edge, j]
            for upward, line, n in terms:
                total = total + beside(upward, j, line) * outer[n, j : j + 1]
            out[j] = total.astype(BF16)

    for turn in range(PEERS):
        row = jnp.bitwise_xor(me, turn)
        pl.when((row >= 2) & (row < 6))(functools.partial(inside, row, outs[turn]))
        for edge, (place, terms) in enumerate(edges):
            pl.when(row == place)(functools.partial(outside, edge, terms, outs[turn]))


def mix_kernel(first, last, source, flux, cloud_top, block, *refs):
    refs = list(refs)
    acc = None if first else refs.pop(0)
    out, weights, wide = refs[:3]
    top = cloud_top[...]
    levels = lax.broadcasted_iota(jnp.int32, (LEVELS, NX), 0)
    inside = levels <= top
    for o in range(LOCAL):
        level = source[0] * LOCAL + o
        kept = jnp.where(inside & (level <= top), flux[level].astype(F32), 0.0)
        weights[o] = kept + jnp.where(levels == level, 1.0, 0.0)
        wide[o] = block[o].astype(F32)
    held = refs[3] if last else out

    def to_out(q):
        span = pl.ds(q * SUB, SUB)
        return pltpu.make_async_copy(held.at[span], out.at[span], refs[4].at[q])

    def some(q, carry):
        row = q * SUB
        for low in range(0, BINS, PART):
            span = slice(low, low + PART)
            sums = [None if first else acc[row + n, span] for n in range(SUB)]
            for o in range(LOCAL):
                data = wide[o, span]
                for n in range(SUB):
                    term = data * weights[o, pl.ds(row + n, 1), :]
                    sums[n] = term if sums[n] is None else sums[n] + term
            for n in range(SUB):
                held[row + n, span] = sums[n]
        if last:
            to_out(q).start()
        return carry

    lax.fori_loop(0, LEVELS // SUB, some, 0)
    if last:

        def finished(q, carry):
            to_out(q).wait()
            return carry

        lax.fori_loop(0, LEVELS // SUB, finished, 0)


def near_core(x):
    return pltpu.with_memory_space_constraint(x, pltpu.VMEM)


VM = pl.BlockSpec(memory_space=pltpu.VMEM)
SM = pl.BlockSpec(memory_space=pltpu.SMEM)
FAR = pl.BlockSpec(memory_space=pltpu.HBM)


def mix(source, flux, cloud_top, block, acc, last):
    first = acc is None
    shape = (LEVELS, BINS, NX)
    scratch = [pltpu.VMEM((LOCAL, LEVELS, NX), F32), pltpu.VMEM((LOCAL, BINS, NX), F32)]
    if last:
        scratch += [pltpu.VMEM(shape, F32), pltpu.SemaphoreType.DMA((LEVELS // SUB,))]
    return pl.pallas_call(
        functools.partial(mix_kernel, first, last),
        out_shape=jax.ShapeDtypeStruct(shape, F32) if last else pltpu.VMEM(shape, F32),
        in_specs=[SM, VM, VM, VM] + ([] if first else [VM]),
        out_specs=FAR if last else VM,
        scratch_shapes=scratch,
        input_output_aliases={} if first or last else {4: 0},
        compiler_params=pltpu.CompilerParams(vmem_limit_bytes=12 << 20),
        cost_estimate=pl.CostEstimate(flops=1_500_000_000, bytes_accessed=7_000_000, transcendentals=0),
        name="mix",
    )(source, near_core(flux), near_core(cloud_top), near_core(block), *([] if first else [acc]))


def swaps(first, count):
    return [pair for i in range(first, count - 1, 2) for pair in ((i, i + 1), (i + 1, i))]


def body(cotangent, particles, coag_rate, courant, offsets, mass_flux, cloud_top):
    forward, inverse = (jnp.asarray(t) for t in tables())
    courant = jnp.moveaxis(courant, 1, 0)
    me = lax.axis_index("lev").astype(jnp.int32)
    params = pltpu.CompilerParams(vmem_limit_bytes=10 << 20)
    half = pltpu.VMEM((LOCAL, BINS, HALF), BF16)
    quarter = pltpu.VMEM((LOCAL, BINS, 256), BF16)
    handed = (
        pltpu.VMEM((2 * BINS, BINS), BF16),
        pltpu.VMEM((BINS, 2 * BINS), BF16),
        pltpu.VMEM((LOCAL, 2, ROWS * NX), F32),
        pltpu.VMEM((2, ROWS * NX), jnp.int32),
    )
    far = functools.partial(pltpu.with_memory_space_constraint, memory_space=pltpu.HBM)
    inputs = [far(x) for x in (coag_rate, forward, inverse, cotangent, particles, courant, offsets)]
    wide, far_rows, near_rows, grad_mid, mass_mid, forward, inverse, courant, offsets = pl.pallas_call(
        edge_kernel,
        out_shape=(pltpu.VMEM((LOCAL, BINS, HALF), F32), quarter, quarter, half, half, *handed),
        in_specs=[FAR] * 7,
        out_specs=(VM,) * 9,
        scratch_shapes=[
            half,
            half,
            pltpu.SMEM((LOCAL,), F32),
            pltpu.SemaphoreType.DMA((LOCAL // STEP, 2, 2)),
            pltpu.SemaphoreType.DMA((3,)),
            pltpu.SemaphoreType.DMA((4,)),
        ],
        compiler_params=params,
        cost_estimate=pl.CostEstimate(flops=600_000_000, bytes_accessed=5_000_000, transcendentals=0),
        name="edge",
    )(*inputs)
    count = lax.axis_size("tile")
    far_rows = lax.ppermute(far_rows, "tile", swaps(1, count))
    near_rows = lax.ppermute(near_rows, "tile", swaps(0, count))
    ready, partial, outer = pl.pallas_call(
        inner_kernel,
        out_shape=(
            pltpu.VMEM((4, LOCAL, BINS, NX), BF16),
            pltpu.VMEM((4, LOCAL, BINS, NX), F32),
            pltpu.VMEM((len(OUTER), LOCAL, NX), F32),
        ),
        in_specs=[SM] + [VM] * 7,
        out_specs=(VM,) * 3,
        scratch_shapes=[pltpu.VMEM((STEP, BINS, HALF), F32)],
        compiler_params=params,
        cost_estimate=pl.CostEstimate(flops=600_000_000, bytes_accessed=8_000_000, transcendentals=0),
        name="inner",
    )(coag_rate, forward, inverse, grad_mid, mass_mid, wide, courant, offsets)
    blocks = pl.pallas_call(
        finish_kernel,
        out_shape=(pltpu.VMEM((LOCAL, BINS, NX), BF16),) * PEERS,
        in_specs=[VM] * 5,
        out_specs=(VM,) * PEERS,
        compiler_params=params,
        cost_estimate=pl.CostEstimate(flops=2_000_000, bytes_accessed=5_000_000, transcendentals=0),
        name="finish",
    )(ready, partial, near_core(far_rows), near_core(near_rows), outer)
    top = cloud_top[None, :]
    arrived = {0: blocks[0]}
    for turn in SENDS:
        arrived[turn] = lax.ppermute(blocks[turn], "lev", [(i, i ^ turn) for i in range(PEERS)])
    acc = None
    for turn in ORDER:
        source = jnp.bitwise_xor(me, turn)[None]
        acc = mix(source, mass_flux, top, arrived[turn], acc, turn == ORDER[-1])
    return acc


def solution(mesh):
    placed = (
        P("lev", None, "tile"),
        P("lev", None, "tile"),
        P("lev"),
        P(None, "lev", "tile"),
        P(None, "tile"),
        P(None, None, ("tile", "lev")),
        P(("tile", "lev")),
    )
    return jax.shard_map(
        body, mesh=mesh, in_specs=placed, out_specs=P(None, None, ("tile", "lev")), check_vma=False
    )
```

```python
import functools
import math

import jax
import jax.numpy as jnp
import ml_dtypes
import numpy as np
from jax import lax
from jax.experimental import pallas as pl
from jax.experimental.pallas import tpu as pltpu
from jax.sharding import PartitionSpec as P

NX = 128
ROWS = 8
REACH = 2
BINS = 96
LOCAL = 9
LEVELS = 72
PEERS = 8
STEP = 3
HALF = 512
SUB = 6
OUTER = ((0, -2), (0, -1), (1, -2), (6, 2), (7, 1), (7, 2))
PART = 48
SENDS = (4, 3, 1, 5, 7, 6, 2)
ORDER = (0, *SENDS)
BF16 = jnp.bfloat16
F32 = jnp.float32


def tables():
    length = 2 * BINS
    freq, bins = np.arange(BINS)[:, None], np.arange(BINS)[None, :]
    theta = 2.0 * math.pi * ((freq * bins) % length) / length
    nyquist = 1.0 - 2.0 * (np.arange(BINS) % 2)
    cos, sin = np.cos(theta), -np.sin(theta)
    sin[0] = nyquist
    forward = np.concatenate([cos, sin], axis=0)
    weight = np.where(np.arange(BINS) == 0, 1.0, 2.0)[:, None] / length
    inverse = np.concatenate([cos * weight, sin * weight], axis=0).T
    return forward.astype(ml_dtypes.bfloat16), np.ascontiguousarray(inverse).astype(ml_dtypes.bfloat16)


def adjoint_of(forward, inverse, gradient, amounts, coefficient):
    grad_spec = jnp.dot(forward, gradient, preferred_element_type=F32)
    mass_spec = jnp.dot(forward, amounts, preferred_element_type=F32)
    grad_re, grad_im = grad_spec[:BINS], grad_spec[BINS:]
    mass_re, mass_im = mass_spec[:BINS], mass_spec[BINS:]
    total_mass = mass_re[0:1]
    first = lax.broadcasted_iota(jnp.int32, (8, gradient.shape[1]), 0) == 0
    re_re, im_im = mass_re * grad_re, mass_im * grad_im
    prod_re = re_re + im_im
    prod_im = mass_re * grad_im - mass_im * grad_re
    prod_re = jnp.concatenate([jnp.where(first, re_re[:8], prod_re[:8]), prod_re[8:]], axis=0)
    prod_im = jnp.concatenate([jnp.where(first, im_im[:8], prod_im[:8]), prod_im[8:]], axis=0)
    prod = jnp.concatenate([prod_re.astype(BF16), prod_im.astype(BF16)], axis=0)
    correlation = jnp.dot(inverse, prod, preferred_element_type=F32)
    grad_wide = gradient.astype(F32)
    inner = jnp.sum(grad_wide * amounts.astype(F32), axis=0, keepdims=True)
    return grad_wide + coefficient * (correlation - grad_wide * total_mass - inner)


def group_copies(pairs, sems, group, low):
    span = pl.ds(group * STEP, STEP)
    width = HALF // len(low)
    return [
        pltpu.make_async_copy(
            source.at[span, :, start : start + width],
            target.at[span, :, side * width : (side + 1) * width],
            sems.at[group, n, side],
        )
        for n, (source, target) in enumerate(pairs)
        for side, start in enumerate(low)
    ]


def begin(copies):
    for copy in copies:
        copy.start()


def finish_copies(copies):
    for copy in copies:
        copy.wait()


def edge_kernel(rate, forward, inverse, cotangent, particles, courant, offsets, *refs):
    wide, far_rows, near_rows, grad_mid, mass_mid, forward_in, inverse_in, courant_in, offsets_in = refs[:9]
    grad, mass, rate_in, sems, small_sems, mid_sems = refs[9:]
    even = lax.rem(lax.axis_index("tile"), 2) == 0
    pairs = ((cotangent, grad), (particles, mass))
    small = [
        pltpu.make_async_copy(source, target, small_sems.at[n])
        for n, (source, target) in enumerate(((rate, rate_in), (forward, forward_in), (inverse, inverse_in)))
    ]
    middle = [
        pltpu.make_async_copy(source, target, mid_sems.at[n])
        for n, (source, target) in enumerate(
            (
                (cotangent.at[:, :, 256:768], grad_mid),
                (particles.at[:, :, 256:768], mass_mid),
                (courant, courant_in),
                (offsets, offsets_in),
            )
        )
    ]
    begin(small + group_copies(pairs, sems, 0, (0, 768)))
    finish_copies(small)

    def some(group, carry):
        finish_copies(group_copies(pairs, sems, group, (0, 768)))

        @pl.when(group < LOCAL // STEP - 1)
        def _():
            begin(group_copies(pairs, sems, group + 1, (0, 768)))

        @pl.when(group == LOCAL // STEP - 2)
        def _():
            begin(middle)

        for j in range(STEP):
            level = group * STEP + j
            adjoint = adjoint_of(forward_in[...], inverse_in[...], grad[level], mass[level], rate_in[level])
            wide[level] = adjoint
            lo, hi = adjoint[:, :256], adjoint[:, 256:]
            far_rows[level] = jnp.where(even, lo, hi).astype(BF16)
            near_rows[level] = jnp.where(even, hi, lo).astype(BF16)
        return carry

    lax.fori_loop(0, LOCAL // STEP, some, 0)
    finish_copies(middle)


def inner_kernel(rate, forward, inverse, cotangent, particles, wide, courant, offsets, ready, partial, outer, cells):
    lane = lax.broadcasted_iota(jnp.int32, (1, NX), 1)
    for n, (row, upwind) in enumerate(OUTER):
        span = slice(row * NX, (row + 1) * NX)
        outer[n] = jnp.where(offsets[0:1, span] == upwind, courant[:, 0, span], 0.0)

    def near(level, j, row):
        if 2 <= row < 6:
            return cells[j, :, (row - 2) * NX : (row - 1) * NX]
        edge = row if row < 2 else row - 4
        return wide[level, :, edge * NX : (edge + 1) * NX]

    def some(group, carry):
        for j in range(STEP):
            level = group * STEP + j
            cells[j] = adjoint_of(forward[...], inverse[...], cotangent[level], particles[level], rate[level])
        for j in range(STEP):
            level = group * STEP + j
            for row in range(ROWS):
                span = slice(row * NX, (row + 1) * NX)
                cour_y, cour_x = courant[level, 0:1, span], courant[level, 1:2, span]
                shift_y, shift_x = offsets[0:1, span], offsets[1:2, span]
                centre = near(level, j, row)
                still = jnp.where(shift_y == 0, cour_y, 0.0)
                total = centre * (1.0 - cour_y - cour_x + still)
                for upwind in (-2, -1, 1, 2):
                    if 0 <= row + upwind < ROWS:
                        weight = jnp.where(shift_y == upwind, cour_y, 0.0)
                        total = total + near(level, j, row + upwind) * weight
                place = lane + shift_x
                weight = jnp.where((place >= 0) & (place < NX), cour_x, 0.0)
                place = jnp.broadcast_to(jnp.clip(place, 0, NX - 1), centre.shape)
                along_x = jnp.take_along_axis(centre, place, axis=1, mode="promise_in_bounds")
                total = total + along_x * weight
                if 2 <= row < 6:
                    ready[row - 2, level] = total.astype(BF16)
                else:
                    partial[row if row < 2 else row - 4, level] = total
        return carry

    lax.fori_loop(0, LOCAL // STEP, some, 0)


def finish_kernel(ready, partial, far_rows, near_rows, outer, *outs):
    me = lax.axis_index("lev")
    even = lax.rem(lax.axis_index("tile"), 2) == 0

    def beside(upward, j, line):
        span = slice(line * NX, (line + 1) * NX)
        return jnp.where(even == upward, far_rows[j, :, span], near_rows[j, :, span]).astype(F32)

    edges = (
        (0, ((True, 0, 0), (True, 1, 1))),
        (1, ((True, 1, 2),)),
        (6, ((False, 0, 3),)),
        (7, ((False, 0, 4), (False, 1, 5))),
    )

    def inside(row, out):
        for j in range(LOCAL):
            out[j] = ready[row - 2, j]

    def outside(edge, terms, out):
        for j in range(LOCAL):
            total = partial[edge, j]
            for upward, line, n in terms:
                total = total + beside(upward, j, line) * outer[n, j : j + 1]
            out[j] = total.astype(BF16)

    for turn in range(PEERS):
        row = jnp.bitwise_xor(me, turn)
        pl.when((row >= 2) & (row < 6))(functools.partial(inside, row, outs[turn]))
        for edge, (place, terms) in enumerate(edges):
            pl.when(row == place)(functools.partial(outside, edge, terms, outs[turn]))


def mix_kernel(first, last, source, flux, cloud_top, block, *refs):
    refs = list(refs)
    acc = None if first else refs.pop(0)
    out, weights, wide = refs[:3]
    top = cloud_top[...]
    levels = lax.broadcasted_iota(jnp.int32, (LEVELS, NX), 0)
    inside = levels <= top
    for o in range(LOCAL):
        level = source[0] * LOCAL + o
        kept = jnp.where(inside & (level <= top), flux[level].astype(F32), 0.0)
        weights[o] = kept + jnp.where(levels == level, 1.0, 0.0)
        wide[o] = block[o].astype(F32)
    held = refs[3] if last else out

    def to_out(q):
        span = pl.ds(q * SUB, SUB)
        return pltpu.make_async_copy(held.at[span], out.at[span], refs[4].at[q])

    def some(q, carry):
        row = q * SUB
        for low in range(0, BINS, PART):
            span = slice(low, low + PART)
            sums = [None if first else acc[row + n, span] for n in range(SUB)]
            for o in range(LOCAL):
                data = wide[o, span]
                for n in range(SUB):
                    term = data * weights[o, pl.ds(row + n, 1), :]
                    sums[n] = term if sums[n] is None else sums[n] + term
            for n in range(SUB):
                held[row + n, span] = sums[n]
        if last:
            to_out(q).start()
        return carry

    lax.fori_loop(0, LEVELS // SUB, some, 0)
    if last:

        def finished(q, carry):
            to_out(q).wait()
            return carry

        lax.fori_loop(0, LEVELS // SUB, finished, 0)


def near_core(x):
    return pltpu.with_memory_space_constraint(x, pltpu.VMEM)


VM = pl.BlockSpec(memory_space=pltpu.VMEM)
SM = pl.BlockSpec(memory_space=pltpu.SMEM)
FAR = pl.BlockSpec(memory_space=pltpu.HBM)


def mix(source, flux, cloud_top, block, acc, last):
    first = acc is None
    shape = (LEVELS, BINS, NX)
    scratch = [pltpu.VMEM((LOCAL, LEVELS, NX), F32), pltpu.VMEM((LOCAL, BINS, NX), F32)]
    if last:
        scratch += [pltpu.VMEM(shape, F32), pltpu.SemaphoreType.DMA((LEVELS // SUB,))]
    return pl.pallas_call(
        functools.partial(mix_kernel, first, last),
        out_shape=jax.ShapeDtypeStruct(shape, F32) if last else pltpu.VMEM(shape, F32),
        in_specs=[SM, VM, VM, VM] + ([] if first else [VM]),
        out_specs=FAR if last else VM,
        scratch_shapes=scratch,
        input_output_aliases={} if first or last else {4: 0},
        compiler_params=pltpu.CompilerParams(vmem_limit_bytes=12 << 20),
        cost_estimate=pl.CostEstimate(flops=1_500_000_000, bytes_accessed=7_000_000, transcendentals=0),
        name="mix",
    )(source, near_core(flux), near_core(cloud_top), near_core(block), *([] if first else [acc]))


def swaps(first, count):
    return [pair for i in range(first, count - 1, 2) for pair in ((i, i + 1), (i + 1, i))]


def body(cotangent, particles, coag_rate, courant, offsets, mass_flux, cloud_top):
    forward, inverse = (jnp.asarray(t) for t in tables())
    courant = jnp.moveaxis(courant, 1, 0)
    me = lax.axis_index("lev").astype(jnp.int32)
    params = pltpu.CompilerParams(vmem_limit_bytes=10 << 20)
    half = pltpu.VMEM((LOCAL, BINS, HALF), BF16)
    quarter = pltpu.VMEM((LOCAL, BINS, 256), BF16)
    handed = (
        pltpu.VMEM((2 * BINS, BINS), BF16),
        pltpu.VMEM((BINS, 2 * BINS), BF16),
        pltpu.VMEM((LOCAL, 2, ROWS * NX), F32),
        pltpu.VMEM((2, ROWS * NX), jnp.int32),
    )
    far = functools.partial(pltpu.with_memory_space_constraint, memory_space=pltpu.HBM)
    inputs = [far(x) for x in (coag_rate, forward, inverse, cotangent, particles, courant, offsets)]
    wide, far_rows, near_rows, grad_mid, mass_mid, forward, inverse, courant, offsets = pl.pallas_call(
        edge_kernel,
        out_shape=(pltpu.VMEM((LOCAL, BINS, HALF), F32), quarter, quarter, half, half, *handed),
        in_specs=[FAR] * 7,
        out_specs=(VM,) * 9,
        scratch_shapes=[
            half,
            half,
            pltpu.SMEM((LOCAL,), F32),
            pltpu.SemaphoreType.DMA((LOCAL // STEP, 2, 2)),
            pltpu.SemaphoreType.DMA((3,)),
            pltpu.SemaphoreType.DMA((4,)),
        ],
        compiler_params=params,
        cost_estimate=pl.CostEstimate(flops=600_000_000, bytes_accessed=5_000_000, transcendentals=0),
        name="edge",
    )(*inputs)
    count = lax.axis_size("tile")
    far_rows = lax.ppermute(far_rows, "tile", swaps(1, count))
    near_rows = lax.ppermute(near_rows, "tile", swaps(0, count))
    ready, partial, outer = pl.pallas_call(
        inner_kernel,
        out_shape=(
            pltpu.VMEM((4, LOCAL, BINS, NX), BF16),
            pltpu.VMEM((4, LOCAL, BINS, NX), F32),
            pltpu.VMEM((len(OUTER), LOCAL, NX), F32),
        ),
        in_specs=[SM] + [VM] * 7,
        out_specs=(VM,) * 3,
        scratch_shapes=[pltpu.VMEM((STEP, BINS, HALF), F32)],
        compiler_params=params,
        cost_estimate=pl.CostEstimate(flops=600_000_000, bytes_accessed=8_000_000, transcendentals=0),
        name="inner",
    )(coag_rate, forward, inverse, grad_mid, mass_mid, wide, courant, offsets)
    blocks = pl.pallas_call(
        finish_kernel,
        out_shape=(pltpu.VMEM((LOCAL, BINS, NX), BF16),) * PEERS,
        in_specs=[VM] * 5,
        out_specs=(VM,) * PEERS,
        compiler_params=params,
        cost_estimate=pl.CostEstimate(flops=2_000_000, bytes_accessed=5_000_000, transcendentals=0),
        name="finish",
    )(ready, partial, near_core(far_rows), near_core(near_rows), outer)
    top = cloud_top[None, :]
    arrived = {0: blocks[0]}
    for turn in SENDS:
        arrived[turn] = lax.ppermute(blocks[turn], "lev", [(i, i ^ turn) for i in range(PEERS)])
    acc = None
    for turn in ORDER:
        source = jnp.bitwise_xor(me, turn)[None]
        acc = mix(source, mass_flux, top, arrived[turn], acc, turn == ORDER[-1])
    return acc


def solution(mesh):
    placed = (
        P("lev", None, "tile"),
        P("lev", None, "tile"),
        P("lev"),
        P(None, "lev", "tile"),
        P(None, "tile"),
        P(None, None, ("tile", "lev")),
        P(("tile", "lev")),
    )
    return jax.shard_map(
        body, mesh=mesh, in_specs=placed, out_specs=P(None, None, ("tile", "lev")), check_vma=False
    )
```

```python
import functools
import math

import jax
import jax.numpy as jnp
import ml_dtypes
import numpy as np
from jax import lax
from jax.experimental import pallas as pl
from jax.experimental.pallas import tpu as pltpu
from jax.sharding import PartitionSpec as P

NX = 128
ROWS = 8
REACH = 2
BINS = 96
LOCAL = 9
LEVELS = 72
PEERS = 8
STEP = 3
HALF = 512
SUB = 6
OUTER = ((0, -2), (0, -1), (1, -2), (6, 2), (7, 1), (7, 2))
PART = 48
SENDS = (4, 3, 1, 5, 7, 6, 2)
ORDER = (0, *SENDS)
BF16 = jnp.bfloat16
F32 = jnp.float32


def tables():
    length = 2 * BINS
    freq, bins = np.arange(BINS)[:, None], np.arange(BINS)[None, :]
    theta = 2.0 * math.pi * ((freq * bins) % length) / length
    nyquist = 1.0 - 2.0 * (np.arange(BINS) % 2)
    cos, sin = np.cos(theta), -np.sin(theta)
    sin[0] = nyquist
    forward = np.concatenate([cos, sin], axis=0)
    weight = np.where(np.arange(BINS) == 0, 1.0, 2.0)[:, None] / length
    inverse = np.concatenate([cos * weight, sin * weight], axis=0).T
    return forward.astype(ml_dtypes.bfloat16), np.ascontiguousarray(inverse).astype(ml_dtypes.bfloat16)


def adjoint_of(forward, inverse, gradient, amounts, coefficient):
    grad_spec = jnp.dot(forward, gradient, preferred_element_type=F32)
    mass_spec = jnp.dot(forward, amounts, preferred_element_type=F32)
    grad_re, grad_im = grad_spec[:BINS], grad_spec[BINS:]
    mass_re, mass_im = mass_spec[:BINS], mass_spec[BINS:]
    total_mass = mass_re[0:1]
    first = lax.broadcasted_iota(jnp.int32, (8, gradient.shape[1]), 0) == 0
    re_re, im_im = mass_re * grad_re, mass_im * grad_im
    prod_re = re_re + im_im
    prod_im = mass_re * grad_im - mass_im * grad_re
    prod_re = jnp.concatenate([jnp.where(first, re_re[:8], prod_re[:8]), prod_re[8:]], axis=0)
    prod_im = jnp.concatenate([jnp.where(first, im_im[:8], prod_im[:8]), prod_im[8:]], axis=0)
    prod = jnp.concatenate([prod_re.astype(BF16), prod_im.astype(BF16)], axis=0)
    correlation = jnp.dot(inverse, prod, preferred_element_type=F32)
    grad_wide = gradient.astype(F32)
    inner = jnp.sum(grad_wide * amounts.astype(F32), axis=0, keepdims=True)
    return grad_wide + coefficient * (correlation - grad_wide * total_mass - inner)


def group_copies(pairs, sems, group, low):
    span = pl.ds(group * STEP, STEP)
    width = HALF // len(low)
    return [
        pltpu.make_async_copy(
            source.at[span, :, start : start + width],
            target.at[span, :, side * width : (side + 1) * width],
            sems.at[group, n, side],
        )
        for n, (source, target) in enumerate(pairs)
        for side, start in enumerate(low)
    ]


def begin(copies):
    for copy in copies:
        copy.start()


def finish_copies(copies):
    for copy in copies:
        copy.wait()


def edge_kernel(rate, forward, inverse, cotangent, particles, courant, offsets, *refs):
    wide, far_rows, near_rows, grad_mid, mass_mid, forward_in, inverse_in, courant_in, offsets_in = refs[:9]
    grad, mass, rate_in, sems, small_sems, mid_sems = refs[9:]
    even = lax.rem(lax.axis_index("tile"), 2) == 0
    pairs = ((cotangent, grad), (particles, mass))
    small = [
        pltpu.make_async_copy(source, target, small_sems.at[n])
        for n, (source, target) in enumerate(((rate, rate_in), (forward, forward_in), (inverse, inverse_in)))
    ]
    middle = [
        pltpu.make_async_copy(source, target, mid_sems.at[n])
        for n, (source, target) in enumerate(
            (
                (cotangent.at[:, :, 256:768], grad_mid),
                (particles.at[:, :, 256:768], mass_mid),
                (courant, courant_in),
                (offsets, offsets_in),
            )
        )
    ]
    begin(group_copies(pairs, sems, 0, (0, 768)) + small)
    finish_copies(small)

    def some(group, carry):
        finish_copies(group_copies(pairs, sems, group, (0, 768)))

        @pl.when(group < LOCAL // STEP - 1)
        def _():
            begin(group_copies(pairs, sems, group + 1, (0, 768)))

        @pl.when(group == LOCAL // STEP - 2)
        def _():
            begin(middle)

        for j in range(STEP):
            level = group * STEP + j
            adjoint = adjoint_of(forward_in[...], inverse_in[...], grad[level], mass[level], rate_in[level])
            wide[level] = adjoint
            lo, hi = adjoint[:, :256], adjoint[:, 256:]
            far_rows[level] = jnp.where(even, lo, hi).astype(BF16)
            near_rows[level] = jnp.where(even, hi, lo).astype(BF16)
        return carry

    lax.fori_loop(0, LOCAL // STEP, some, 0)
    finish_copies(middle)


def inner_kernel(rate, forward, inverse, cotangent, particles, wide, courant, offsets, ready, partial, outer, cells):
    lane = lax.broadcasted_iota(jnp.int32, (1, NX), 1)
    for n, (row, upwind) in enumerate(OUTER):
        span = slice(row * NX, (row + 1) * NX)
        outer[n] = jnp.where(offsets[0:1, span] == upwind, courant[:, 0, span], 0.0)

    def near(level, j, row):
        if 2 <= row < 6:
            return cells[j, :, (row - 2) * NX : (row - 1) * NX]
        edge = row if row < 2 else row - 4
        return wide[level, :, edge * NX : (edge + 1) * NX]

    def some(group, carry):
        for j in range(STEP):
            level = group * STEP + j
            cells[j] = adjoint_of(forward[...], inverse[...], cotangent[level], particles[level], rate[level])
        for j in range(STEP):
            level = group * STEP + j
            for row in range(ROWS):
                span = slice(row * NX, (row + 1) * NX)
                cour_y, cour_x = courant[level, 0:1, span], courant[level, 1:2, span]
                shift_y, shift_x = offsets[0:1, span], offsets[1:2, span]
                centre = near(level, j, row)
                still = jnp.where(shift_y == 0, cour_y, 0.0)
                total = centre * (1.0 - cour_y - cour_x + still)
                for upwind in (-2, -1, 1, 2):
                    if 0 <= row + upwind < ROWS:
                        weight = jnp.where(shift_y == upwind, cour_y, 0.0)
                        total = total + near(level, j, row + upwind) * weight
                place = lane + shift_x
                weight = jnp.where((place >= 0) & (place < NX), cour_x, 0.0)
                place = jnp.broadcast_to(jnp.clip(place, 0, NX - 1), centre.shape)
                along_x = jnp.take_along_axis(centre, place, axis=1, mode="promise_in_bounds")
                total = total + along_x * weight
                if 2 <= row < 6:
                    ready[row - 2, level] = total.astype(BF16)
                else:
                    partial[row if row < 2 else row - 4, level] = total
        return carry

    lax.fori_loop(0, LOCAL // STEP, some, 0)


def finish_kernel(ready, partial, far_rows, near_rows, outer, *outs):
    me = lax.axis_index("lev")
    even = lax.rem(lax.axis_index("tile"), 2) == 0

    def beside(upward, j, line):
        span = slice(line * NX, (line + 1) * NX)
        return jnp.where(even == upward, far_rows[j, :, span], near_rows[j, :, span]).astype(F32)

    edges = (
        (0, ((True, 0, 0), (True, 1, 1))),
        (1, ((True, 1, 2),)),
        (6, ((False, 0, 3),)),
        (7, ((False, 0, 4), (False, 1, 5))),
    )

    def inside(row, out):
        for j in range(LOCAL):
            out[j] = ready[row - 2, j]

    def outside(edge, terms, out):
        for j in range(LOCAL):
            total = partial[edge, j]
            for upward, line, n in terms:
                total = total + beside(upward, j, line) * outer[n, j : j + 1]
            out[j] = total.astype(BF16)

    for turn in range(PEERS):
        row = jnp.bitwise_xor(me, turn)
        pl.when((row >= 2) & (row < 6))(functools.partial(inside, row, outs[turn]))
        for edge, (place, terms) in enumerate(edges):
            pl.when(row == place)(functools.partial(outside, edge, terms, outs[turn]))


def mix_kernel(first, last, source, flux, cloud_top, block, *refs):
    refs = list(refs)
    acc = None if first else refs.pop(0)
    out, weights, wide = refs[:3]
    top = cloud_top[...]
    levels = lax.broadcasted_iota(jnp.int32, (LEVELS, NX), 0)
    inside = levels <= top
    for o in range(LOCAL):
        level = source[0] * LOCAL + o
        kept = jnp.where(inside & (level <= top), flux[level].astype(F32), 0.0)
        weights[o] = kept + jnp.where(levels == level, 1.0, 0.0)
        wide[o] = block[o].astype(F32)
    held = refs[3] if last else out

    def to_out(q):
        span = pl.ds(q * SUB, SUB)
        return pltpu.make_async_copy(held.at[span], out.at[span], refs[4].at[q])

    def some(q, carry):
        row = q * SUB
        for low in range(0, BINS, PART):
            span = slice(low, low + PART)
            sums = [None if first else acc[row + n, span] for n in range(SUB)]
            for o in range(LOCAL):
                data = wide[o, span]
                for n in range(SUB):
                    term = data * weights[o, pl.ds(row + n, 1), :]
                    sums[n] = term if sums[n] is None else sums[n] + term
            for n in range(SUB):
                held[row + n, span] = sums[n]
        if last:
            to_out(q).start()
        return carry

    lax.fori_loop(0, LEVELS // SUB, some, 0, unroll=2)
    if last:

        def finished(q, carry):
            to_out(q).wait()
            return carry

        lax.fori_loop(0, LEVELS // SUB, finished, 0)


def near_core(x):
    return pltpu.with_memory_space_constraint(x, pltpu.VMEM)


VM = pl.BlockSpec(memory_space=pltpu.VMEM)
SM = pl.BlockSpec(memory_space=pltpu.SMEM)
FAR = pl.BlockSpec(memory_space=pltpu.HBM)


def mix(source, flux, cloud_top, block, acc, last):
    first = acc is None
    shape = (LEVELS, BINS, NX)
    scratch = [pltpu.VMEM((LOCAL, LEVELS, NX), F32), pltpu.VMEM((LOCAL, BINS, NX), F32)]
    if last:
        scratch += [pltpu.VMEM(shape, F32), pltpu.SemaphoreType.DMA((LEVELS // SUB,))]
    return pl.pallas_call(
        functools.partial(mix_kernel, first, last),
        out_shape=jax.ShapeDtypeStruct(shape, F32) if last else pltpu.VMEM(shape, F32),
        in_specs=[SM, VM, VM, VM] + ([] if first else [VM]),
        out_specs=FAR if last else VM,
        scratch_shapes=scratch,
        input_output_aliases={} if first or last else {4: 0},
        compiler_params=pltpu.CompilerParams(vmem_limit_bytes=12 << 20),
        cost_estimate=pl.CostEstimate(flops=1_500_000_000, bytes_accessed=7_000_000, transcendentals=0),
        name="mix",
    )(source, near_core(flux), near_core(cloud_top), near_core(block), *([] if first else [acc]))


def swaps(first, count):
    return [pair for i in range(first, count - 1, 2) for pair in ((i, i + 1), (i + 1, i))]


def body(cotangent, particles, coag_rate, courant, offsets, mass_flux, cloud_top):
    forward, inverse = (jnp.asarray(t) for t in tables())
    courant = jnp.moveaxis(courant, 1, 0)
    me = lax.axis_index("lev").astype(jnp.int32)
    params = pltpu.CompilerParams(vmem_limit_bytes=10 << 20)
    half = pltpu.VMEM((LOCAL, BINS, HALF), BF16)
    quarter = pltpu.VMEM((LOCAL, BINS, 256), BF16)
    handed = (
        pltpu.VMEM((2 * BINS, BINS), BF16),
        pltpu.VMEM((BINS, 2 * BINS), BF16),
        pltpu.VMEM((LOCAL, 2, ROWS * NX), F32),
        pltpu.VMEM((2, ROWS * NX), jnp.int32),
    )
    far = functools.partial(pltpu.with_memory_space_constraint, memory_space=pltpu.HBM)
    inputs = [far(x) for x in (coag_rate, forward, inverse, cotangent, particles, courant, offsets)]
    wide, far_rows, near_rows, grad_mid, mass_mid, forward, inverse, courant, offsets = pl.pallas_call(
        edge_kernel,
        out_shape=(pltpu.VMEM((LOCAL, BINS, HALF), F32), quarter, quarter, half, half, *handed),
        in_specs=[FAR] * 7,
        out_specs=(VM,) * 9,
        scratch_shapes=[
            half,
            half,
            pltpu.SMEM((LOCAL,), F32),
            pltpu.SemaphoreType.DMA((LOCAL // STEP, 2, 2)),
            pltpu.SemaphoreType.DMA((3,)),
            pltpu.SemaphoreType.DMA((4,)),
        ],
        compiler_params=params,
        cost_estimate=pl.CostEstimate(flops=600_000_000, bytes_accessed=5_000_000, transcendentals=0),
        name="edge",
    )(*inputs)
    count = lax.axis_size("tile")
    far_rows = lax.ppermute(far_rows, "tile", swaps(1, count))
    near_rows = lax.ppermute(near_rows, "tile", swaps(0, count))
    ready, partial, outer = pl.pallas_call(
        inner_kernel,
        out_shape=(
            pltpu.VMEM((4, LOCAL, BINS, NX), BF16),
            pltpu.VMEM((4, LOCAL, BINS, NX), F32),
            pltpu.VMEM((len(OUTER), LOCAL, NX), F32),
        ),
        in_specs=[SM] + [VM] * 7,
        out_specs=(VM,) * 3,
        scratch_shapes=[pltpu.VMEM((STEP, BINS, HALF), F32)],
        compiler_params=params,
        cost_estimate=pl.CostEstimate(flops=600_000_000, bytes_accessed=8_000_000, transcendentals=0),
        name="inner",
    )(coag_rate, forward, inverse, grad_mid, mass_mid, wide, courant, offsets)
    blocks = pl.pallas_call(
        finish_kernel,
        out_shape=(pltpu.VMEM((LOCAL, BINS, NX), BF16),) * PEERS,
        in_specs=[VM] * 5,
        out_specs=(VM,) * PEERS,
        compiler_params=params,
        cost_estimate=pl.CostEstimate(flops=2_000_000, bytes_accessed=5_000_000, transcendentals=0),
        name="finish",
    )(ready, partial, near_core(far_rows), near_core(near_rows), outer)
    top = cloud_top[None, :]
    arrived = {0: blocks[0]}
    for turn in SENDS:
        arrived[turn] = lax.ppermute(blocks[turn], "lev", [(i, i ^ turn) for i in range(PEERS)])
    acc = None
    for turn in ORDER:
        source = jnp.bitwise_xor(me, turn)[None]
        acc = mix(source, mass_flux, top, arrived[turn], acc, turn == ORDER[-1])
    return acc


def solution(mesh):
    placed = (
        P("lev", None, "tile"),
        P("lev", None, "tile"),
        P("lev"),
        P(None, "lev", "tile"),
        P(None, "tile"),
        P(None, None, ("tile", "lev")),
        P(("tile", "lev")),
    )
    return jax.shard_map(
        body, mesh=mesh, in_specs=placed, out_specs=P(None, None, ("tile", "lev")), check_vma=False
    )
```
